32 devices in a mesh: dp: 8 (over y, x, core), tensor: 4 (over z).
Axes of the slice: x: 2, y: 2, z: 4, core: 2. Of those that a mesh axis runs over, the one named last changes fastest.
Arguments:
- acts: bfloat16 [256, 4096], P(('dp', 'tensor')), may hold values from -6 to 6
- gate_pre: bfloat16 [256, 14336], P('dp', 'tensor'), may hold values from -8 to 8
- up_pre: bfloat16 [256, 14336], P('dp', 'tensor'), may hold values from -6 to 6
- out_grad: bfloat16 [256, 4096], P(('dp', 'tensor')), may hold values from -6 to 6
- segments: int32 [8, 32], P('dp', 'tensor'), may hold values from 0 to 23, never falling along the last dimension, each value on 1 to 8 neighbouring positions
- down_weight: bfloat16 [4096, 14336], P(None, 'tensor'), may hold values from -0.046875 to 0.046875
Outputs:
- grad_gate: float32 [4096, 14336], P('dp', 'tensor')
- grad_up: float32 [4096, 14336], P('dp', 'tensor')
- grad_down: float32 [4096, 14336], P('dp', 'tensor')
The draws below stay inside these ranges and needn't reach their ends.
Inputs may be any that keep to these rules, and one draw needn't show every extreme that they name: `segments`: within each group ids never fall; each id that occurs covers 1 to 8 tokens, and some id covers exactly that many.
All inputs are finite; a program needn't handle non-finite values.
Results may differ from the reference program's by a relative error of at most 0.014.
Values may be sent and summed in bfloat16 or wider, within the bound.
A program may use at most 256 MiB of HBM per device.

```python
import math
import jax
import jax.numpy as jnp
import numpy as np
from jax import lax

D = 4096
FF = 14336
SEGS = 24
TOK_GROUP = 32
TOKENS = 256
N_DP = 8


def with_spikes(result, rng, source, target, blocks, factor):
    owner, partner = [(jnp.arange(result.shape[axis_at]) // (result.shape[axis_at] // blocks)).reshape([-1 if axis == axis_at else 1 for axis in range(result.ndim)]) for axis_at in (source, target)]
    chosen = jax.random.permutation(rng, blocks)[partner]
    strong = (owner == chosen) | (owner == (partner + blocks // 2) % blocks)
    return jnp.where(strong, factor * result, result)


def block_scale(key, extent, pieces, smallest, top_value):
    def one(axis_at, shards_of):
        heights = jax.random.uniform(jax.random.fold_in(jax.random.fold_in(key, 6), axis_at), (shards_of,), jnp.float32, smallest / len(pieces), top_value / len(pieces))
        return jnp.repeat(jnp.exp(heights), extent[axis_at] // shards_of).reshape((-1,) + (1,) * (len(extent) - axis_at - 1))

    gain = one(*pieces[0])
    for cut in pieces[1:]:
        gain = gain * one(*cut)
    return gain


def length_profile(count, total, reach, slope):
    loads = [(1 << 20) // math.isqrt(standing ** slope) + 1 for standing in range(2, count + 1)]
    rest, given = total - reach - (count - 1), [1] * (count - 1)
    while rest > 0:
        movable = [i for i in range(count - 1) if given[i] < reach]
        mass, left = sum([loads[i] for i in movable]), rest
        for i in movable:
            more = min(reach - given[i], max(1, left * loads[i] // mass), rest)
            given[i] = given[i] + more
            rest = rest - more
    return np.array([reach] + given)


def ragged_sizes(key, number_of, total, bound, lean):
    if number_of == 2:
        one = jax.random.randint(key, (), max(1, total - bound), min(bound, total - 1) + 1)
        return jnp.stack([one, total - one])
    lengths = jnp.asarray(length_profile(number_of, total, bound, lean), jnp.int32)
    twos = (number_of - 1) // 2
    source_of, sink = lengths[1:1 + 2 * twos:2], lengths[2:2 + 2 * twos:2]
    margin = jnp.minimum(source_of - 1, bound - sink)
    passed = jax.random.randint(jax.random.fold_in(key, 1), (twos,), 0, 1 << 20) % (margin + 1)
    lengths = lengths.at[1:1 + 2 * twos:2].set(source_of - passed).at[2:2 + 2 * twos:2].set(sink + passed)
    return lengths[jax.random.permutation(jax.random.fold_in(key, 2), number_of)]


def bell_draw(rng, shape, deviation, most, shards=(), kind=jnp.bfloat16):
    gain = block_scale(rng, shape, shards, -0.22, 0.18) if shards else 1.0
    values = jax.random.normal(rng, shape, jnp.float32) * deviation * gain
    return jnp.minimum(jnp.maximum(values, -most), most).astype(kind)


def bell_draw_with(key, shape, scale, most, pieces, heavy, held_as=jnp.bfloat16):
    drawn = scale * jax.random.normal(key, shape, jnp.float32)
    if pieces:
        drawn = drawn * block_scale(key, shape, pieces, -0.22, 0.18)
    return jnp.clip(with_spikes(drawn, jax.random.fold_in(key, 3), *heavy), -most, most).astype(held_as)


def setup_inputs(seed: int = 0) -> dict:
    streams_of = jax.random.split(jax.random.key(seed), 7)
    acts = bell_draw(streams_of[0], (TOKENS, D), 1.0, 6.0, ((0, 32),))
    gate_pre = bell_draw(streams_of[1], (TOKENS, FF), 1.5, 8.0, ((0, 8), (1, 4)))
    up_pre = bell_draw(streams_of[2], (TOKENS, FF), 1.0, 6.0, ((0, 8), (1, 4)))
    out_grad = bell_draw_with(streams_of[3], (TOKENS, D), 1.0, 6.0, ((0, 32),), (0, 1, 32, 2.75))
    segments = jax.vmap(lambda own: jnp.searchsorted(jnp.cumsum(ragged_sizes(own, SEGS, TOK_GROUP, TOK_GROUP // 4, 1)), jnp.arange(TOK_GROUP), side="right"))(jax.random.split(streams_of[4], N_DP)).reshape((N_DP, TOK_GROUP)).astype(jnp.int32)
    down_weight = bell_draw(streams_of[5], (D, FF), FF ** -0.5, 0.046875, ((1, 4),))
    return dict(acts=acts, gate_pre=gate_pre, up_pre=up_pre, out_grad=out_grad, segments=segments, down_weight=down_weight)


def token_weights(seg_ids):
    table = jnp.arange(SEGS, dtype=jnp.int32)
    onehot = (seg_ids[:, None] == table[None, :]).astype(jnp.float32)
    counts = jnp.sum(onehot, axis=0)
    own = jnp.sum(onehot * counts[None, :], axis=1)
    return 1.0 / own


def rounded(value):
    return lax.optimization_barrier(value.astype(jnp.bfloat16)).astype(jnp.float32)


def reference(acts, gate_pre, up_pre, out_grad, segments, down_weight):
    inputs = acts.reshape(N_DP, TOK_GROUP, D)
    grads = out_grad.reshape(N_DP, TOK_GROUP, D)
    gates = gate_pre.reshape(N_DP, TOK_GROUP, FF)
    ups = up_pre.reshape(N_DP, TOK_GROUP, FF)

    def one_group(carry, item):
        x_rows, dy_rows, g_rows, u_rows, seg_rows = item
        weights = token_weights(seg_rows)
        gate = g_rows.astype(jnp.float32)
        up = u_rows.astype(jnp.float32)
        sigma = jax.nn.sigmoid(gate)
        active = gate * sigma
        hidden_grad = weights[:, None] * jnp.dot(dy_rows, down_weight, preferred_element_type=jnp.float32)
        gate_grad = (hidden_grad * up * sigma * (1.0 + gate * (1.0 - sigma))).astype(jnp.bfloat16)
        up_grad = (hidden_grad * active).astype(jnp.bfloat16)
        weighted_hidden = (weights[:, None] * active * up).astype(jnp.bfloat16)
        part_gate = rounded(jnp.dot(x_rows.T, gate_grad, preferred_element_type=jnp.float32))
        part_up = rounded(jnp.dot(x_rows.T, up_grad, preferred_element_type=jnp.float32))
        part_down = rounded(jnp.dot(dy_rows.T, weighted_hidden, preferred_element_type=jnp.float32))
        return (carry[0] + part_gate, carry[1] + part_up, carry[2] + part_down), None

    zeros = jnp.zeros((D, FF), jnp.float32)
    totals, unused = lax.scan(one_group, (zeros, zeros, zeros), (inputs, grads, gates, ups, segments))
    return (totals[0], totals[1], totals[2])
```

```python
import jax
import jax.numpy as jnp
from jax import lax
from jax.sharding import PartitionSpec as P

MESH = ("dp", "tensor")


def contract(left, right):
    return lax.dot_general(
        left, right, (((0,), (0,)), ((), ())), preferred_element_type=jnp.float32
    )


def token_weights(seg_groups):
    same = seg_groups[:, :, None] == seg_groups[:, None, :]
    return 1.0 / jnp.sum(same.astype(jnp.float32), axis=2).reshape(-1)


def body(acts, gate_pre, up_pre, out_grad, segments, down_weight):
    n_dp, n_t = lax.axis_size("dp"), lax.axis_size("tensor")
    rows, d = acts.shape
    grad_all = lax.all_gather(out_grad, MESH, axis=0, tiled=True)
    gate_all = lax.all_gather(gate_pre, "dp", axis=0, tiled=True)
    up_all = lax.all_gather(up_pre, "dp", axis=0, tiled=True)
    seg_all = lax.all_gather(segments, MESH, axis=0, tiled=True)
    seg_all = seg_all.reshape(n_dp, n_t * rows)
    cols = d // n_dp
    mine = lax.all_to_all(acts, "dp", split_axis=1, concat_axis=0, tiled=True)
    mine = lax.all_gather(mine, "tensor", axis=0, tiled=False)
    mine = mine.reshape(n_t, n_dp, rows, cols).transpose(1, 0, 2, 3).reshape(-1, cols)
    me = lax.axis_index("dp")
    grad_mine = lax.dynamic_slice_in_dim(grad_all, me * cols, cols, axis=1)
    weights = token_weights(seg_all)[:, None]
    raw = jnp.dot(grad_all, down_weight, preferred_element_type=jnp.float32)
    gate = gate_all.astype(jnp.float32)
    up = up_all.astype(jnp.float32)
    sigma = jax.nn.sigmoid(gate)
    active = gate * sigma
    hidden_grad = weights * raw
    gate_grad = (hidden_grad * up * sigma * (1.0 + gate * (1.0 - sigma))).astype(jnp.bfloat16)
    up_grad = (hidden_grad * active).astype(jnp.bfloat16)
    weighted_hidden = (weights * active * up).astype(jnp.bfloat16)
    return contract(mine, gate_grad), contract(mine, up_grad), contract(grad_mine, weighted_hidden)


def solution(mesh):
    in_specs = (
        P(("dp", "tensor"), None),
        P("dp", "tensor"),
        P("dp", "tensor"),
        P(("dp", "tensor"), None),
        P("dp", "tensor"),
        P(None, "tensor"),
    )
    out_specs = (P("dp", "tensor"), P("dp", "tensor"), P("dp", "tensor"))
    return jax.shard_map(body, mesh=mesh, in_specs=in_specs, out_specs=out_specs, check_vma=False)
```

```python
import functools

import jax
import jax.numpy as jnp
from jax import lax
from jax.experimental import pallas as pl
from jax.experimental.pallas import tpu as pltpu
from jax.sharding import PartitionSpec as P

MESH = ("dp", "tensor")
F32, BF16 = jnp.float32, jnp.bfloat16
CORE, NEAR, FAR = 1, 2, 4


def tile_of(extent, most):
    return max(t for t in range(128, most + 1, 128) if extent % t == 0)


def hidden_kernel(
    n_dp, n_t,
    acts, grads, segs, gate_in, up_in, weight_in,
    gg_out, ug_out, wh_out, acts_t_out, grads_t_out,
    og, acts_cut, ac, sg, gu, wt, acc, lhs32, lhs16, own32, sg32, wgt,
    og_s, og_r, line_s, line_r, sib_s, sib_r, cut_s, cut_r, cl_s, cl_r, gu_s, gu_r, w_sem, own_sem,
):
    chips = n_dp // 2
    nk = chips
    rows, d = acts.shape
    dk = d // nk
    half = dk // 2
    group = n_t * rows
    ff = gate_in.shape[1]
    nf = gu.shape[1]
    fcut = ff // nf
    dp, z = lax.axis_index("dp"), lax.axis_index("tensor")
    core, chip = dp % 2, dp // 2

    def send(src, dst, s, r, to_dp, to_z):
        pltpu.make_async_remote_copy(
            src_ref=src, dst_ref=dst, send_sem=s, recv_sem=r,
            device_id=(to_dp, to_z), device_id_type=pl.DeviceIdType.MESH,
        ).start()

    def desc(ref, s, r):
        return pltpu.make_async_remote_copy(
            src_ref=ref, dst_ref=ref, send_sem=s, recv_sem=r,
            device_id=(dp ^ CORE, z), device_id_type=pl.DeviceIdType.MESH,
        )

    barrier = pltpu.get_barrier_semaphore()
    for rel in range(1, n_dp):
        pl.semaphore_signal(barrier, inc=1, device_id=(dp ^ rel, z), device_id_type=pl.DeviceIdType.MESH)

    @pl.when(z > 0)
    def _():
        pl.semaphore_signal(barrier, inc=1, device_id=(dp, z - 1), device_id_type=pl.DeviceIdType.MESH)

    @pl.when(z < n_t - 1)
    def _():
        pl.semaphore_signal(barrier, inc=1, device_id=(dp, z + 1), device_id_type=pl.DeviceIdType.MESH)

    w_copies = [
        pltpu.make_async_copy(weight_in.at[pl.ds(k * dk, dk)], wt.at[pl.ds(k * dk, dk)], w_sem.at[k])
        for k in range(nk)
    ]
    for c in w_copies:
        c.start()
    gu_in = (gate_in, up_in)
    own_copies = []
    for j in range(2):
        for f in range(nf):
            c = pltpu.make_async_copy(gu_in[j].at[:, pl.ds(f * fcut, fcut)], gu.at[j, f, dp], own_sem.at[j, f])
            c.start()
            own_copies.append(c)

    def stacked(x):
        w = x.shape[1] // 2
        return jnp.concatenate([x[:, :w], x[:, w:]], axis=0).astype(BF16)

    for k in range(nk):
        og[k, core, z, chip] = stacked(grads[:, k * dk:(k + 1) * dk].astype(F32))
    cols = d // n_dp
    for i in range(n_dp):
        acts_cut[i] = stacked(acts[:, i * cols:(i + 1) * cols].astype(F32))
    ac[z, dp] = acts_cut[dp]
    seg_row = jnp.broadcast_to(segs[...], (rows, rows))
    diag = lax.broadcasted_iota(jnp.int32, (rows, rows), 0) == lax.broadcasted_iota(jnp.int32, (rows, rows), 1)
    seg_col = jnp.sum(jnp.where(diag, seg_row, 0), axis=1, keepdims=True)
    sg[z, dp] = jnp.broadcast_to(seg_col, (rows, 128))

    pl.semaphore_wait(barrier, n_dp - 1 + (z > 0).astype(jnp.int32) + (z < n_t - 1).astype(jnp.int32))

    for k in range(nk):
        for rel in range(1, chips):
            mine = og.at[k, core, z, chip]
            send(mine, mine, og_s.at[k, rel], og_r.at[k, rel], dp ^ (2 * rel), z)

    def gu_axes(j):
        return (NEAR, FAR) if j == 0 else (FAR, NEAR)

    def start_gu():
        for f in range(nf):
            for j in range(2):
                own_copies[j * nf + f].wait()
            for t in range(2):
                for j in range(2):
                    mine = gu.at[j, f, dp]
                    send(mine, mine, gu_s.at[j, f, t], gu_r.at[j, f, t], dp ^ gu_axes(j)[t], z)
            for j in range(2):
                mine = gu.at[j, f, dp]
                send(mine, mine, gu_s.at[j, f, 3], gu_r.at[j, f, 3], dp ^ CORE, z)

    def gu_hop(j, f, t):
        a, b = gu_axes(j)
        slot = gu.at[j, f, dp ^ (a, b, a ^ b)[t]]
        desc(slot, gu_s.at[j, f, t], gu_r.at[j, f, t]).wait_recv()
        if t == 0:
            send(slot, slot, gu_s.at[j, f, 2], gu_r.at[j, f, 2], dp ^ b, z)
        send(slot, slot, gu_s.at[j, f, 4 + t], gu_r.at[j, f, 4 + t], dp ^ CORE, z)

    def start_cut():
        for rel in range(1, n_dp):
            send(acts_cut.at[dp ^ rel], ac.at[z, dp], cut_s.at[0, rel], cut_r.at[0, rel], dp ^ rel, z)
            send(sg.at[z, dp], sg.at[z, dp], cut_s.at[1, rel], cut_r.at[1, rel], dp ^ rel, z)

    def line_parts(k):
        if k < nk:
            return [(lambda s: og.at[k, core, s], line_s.at[k], line_r.at[k])]
        return [(lambda s: ac.at[s], cl_s.at[0], cl_r.at[0]), (lambda s: sg.at[s], cl_s.at[1], cl_r.at[1])]

    def pass_on(k, s):
        if k < nk:
            plane = og.at[k, core, s]
            send(plane, plane, sib_s.at[k, s], sib_r.at[k, s], dp ^ CORE, z)

    def step(k, h):
        if h == 0:
            if k < nk:
                for rel in range(1, chips):
                    desc(og.at[k, core, z, chip ^ rel], og_s.at[k, rel], og_r.at[k, rel]).wait_recv()
            else:
                for rel in range(1, n_dp):
                    desc(ac.at[z, dp ^ rel], cut_s.at[0, rel], cut_r.at[0, rel]).wait_recv()
                    desc(sg.at[z, dp ^ rel], cut_s.at[1, rel], cut_r.at[1, rel]).wait_recv()
        for way in range(2):
            sign = 1 - 2 * way
            src = z - sign * h
            nxt = z + sign
            valid = (src >= 0) & (src < n_t)

            def arrive(way=way, src=src, nxt=nxt):
                if h:
                    for at, s, r in line_parts(k):
                        desc(at(src), s.at[way, h], r.at[way, h]).wait_recv()

                if h + 1 < n_t:
                    @pl.when((nxt >= 0) & (nxt < n_t))
                    def _():
                        for at, s, r in line_parts(k):
                            send(at(src), at(src), s.at[way, h + 1], r.at[way, h + 1], dp, nxt)

                if h or way == 0:
                    pass_on(k, src)

            if h:
                pl.when(valid)(arrive)
            else:
                arrive()

    tf = tile_of(ff, 512)

    def matmul(k):
        for s in range(n_t):
            desc(og.at[k, 1 - core, s], sib_s.at[k, s], sib_r.at[k, s]).wait_recv()

        def unpack(i, carry):
            c, s, q = i // (n_t * chips), (i // chips) % n_t, i % chips
            x = og[k, c, s, q].astype(F32)
            to = (q * 2 + c) * n_t + s
            lhs32[to, :, 0:half] = x[:rows]
            lhs32[to, :, half:dk] = x[rows:]
            return carry

        lax.fori_loop(0, n_dp * n_t, unpack, 0)
        lhs16[...] = lhs32[...].reshape(n_dp * group, dk).astype(BF16)

        @pl.when(dp // 2 == k)
        def _():
            own32[...] = lhs32[:, :, pl.ds(pl.multiple_of((dp % 2) * half, half), half)].reshape(n_dp * group, half)

        w_copies[k].wait()

        def one(t, carry):
            at = pl.ds(pl.multiple_of(t * tf, tf), tf)
            part = jnp.dot(lhs16[...], wt[pl.ds(k * dk, dk), at], preferred_element_type=F32)
            if k == 0:
                acc[:, at] = part
            else:
                acc[:, at] += part
            return carry

        lax.fori_loop(0, ff // tf, one, 0)

    start_gu()
    start_cut()
    for s in range(nk + n_t):
        for h in range(n_t):
            if 0 <= s - h <= nk:
                step(s - h, h)
        if s == n_t - 1:
            for f in range(nf):
                for j in range(2):
                    gu_hop(j, f, 0)
        if s == n_t:
            for f in range(nf):
                for j in range(2):
                    gu_hop(j, f, 1)
        if 0 <= s - (n_t - 1) < nk:
            matmul(s - (n_t - 1))
    grads_t_out[...] = own32[...].T.astype(BF16)

    def unpack_cut(i, carry):
        s, g = i // n_dp, i % n_dp
        x = ac[s, g].astype(F32)
        to = g * n_t + s
        lhs32[to, :, 0:cols // 2] = x[:rows]
        lhs32[to, :, cols // 2:cols] = x[rows:]
        sg32[to] = sg[s, g]
        return carry

    lax.fori_loop(0, n_dp * n_t, unpack_cut, 0)
    acts_t_out[...] = lhs32[:, :, 0:cols].reshape(n_dp * group, cols).T.astype(BF16)

    eye = lax.broadcasted_iota(jnp.int32, (group, group), 0) == lax.broadcasted_iota(jnp.int32, (group, group), 1)
    per = group // rows

    def weigh(g, carry):
        seg = sg32[pl.ds(g * per, per)].reshape(group, 128)[:, 0:1]
        wide = jnp.broadcast_to(seg, (group, group))
        row = jnp.sum(jnp.where(eye, wide, 0), axis=0, keepdims=True)
        count = jnp.sum((wide == row).astype(F32), axis=1, keepdims=True)
        wgt[g] = jnp.broadcast_to(1.0 / count, (group, 128))
        return carry

    lax.fori_loop(0, n_dp, weigh, 0)

    for f in range(nf):
        for j in range(2):
            gu_hop(j, f, 2)
    for f in range(nf):
        for j in range(2):
            a, b = gu_axes(j)
            for t, slot in ((3, 0), (4, a), (5, b), (6, a ^ b)):
                desc(gu.at[j, f, dp ^ CORE ^ slot], gu_s.at[j, f, t], gu_r.at[j, f, t]).wait_recv()
    te = tile_of(fcut, 512)
    for f in range(nf):
        def element(i, carry, f=f):
            g, t = i // (fcut // te), i % (fcut // te)
            at = pl.ds(pl.multiple_of(t * te, te), te)
            here = pl.ds(pl.multiple_of(f * fcut + t * te, te), te)
            rows_at = pl.ds(pl.multiple_of(g * group, group), group)
            gate = gu[0, f, g, :, at].astype(F32)
            up = gu[1, f, g, :, at].astype(F32)
            w = wgt[g][:, 0:1]
            raw = acc[rows_at, here]
            sigma = jax.nn.sigmoid(gate)
            active = gate * sigma
            hid = w * raw
            gg_out[rows_at, here] = (hid * up * (sigma + active * (1.0 - sigma))).astype(BF16)
            ug_out[rows_at, here] = (hid * active).astype(BF16)
            wh_out[rows_at, here] = (w * active * up).astype(BF16)
            return carry

        lax.fori_loop(0, n_dp * (fcut // te), element, 0)

    for k in range(nk):
        for rel in range(1, chips):
            desc(og.at[k, core, z, chip], og_s.at[k, rel], og_r.at[k, rel]).wait_send()
        for s in range(n_t):
            desc(og.at[k, core, s], sib_s.at[k, s], sib_r.at[k, s]).wait_send()
    for rel in range(1, n_dp):
        desc(acts_cut.at[dp ^ rel], cut_s.at[0, rel], cut_r.at[0, rel]).wait_send()
        desc(sg.at[z, dp], cut_s.at[1, rel], cut_r.at[1, rel]).wait_send()
    for k in range(nk + 1):
        for h in range(1, n_t):
            for way in range(2):
                sign = 1 - 2 * way
                src, nxt = z - sign * (h - 1), z + sign

                @pl.when((src >= 0) & (src < n_t) & (nxt >= 0) & (nxt < n_t))
                def _():
                    for at, s, r in line_parts(k):
                        desc(at(src), s.at[way, h], r.at[way, h]).wait_send()
    for f in range(nf):
        for j in range(2):
            for t in range(7):
                desc(gu.at[j, f, dp], gu_s.at[j, f, t], gu_r.at[j, f, t]).wait_send()


def hidden_call(n_dp, n_t, acts, gate_pre, up_pre, out_grad, segments, down_weight):
    rows, d = acts.shape
    group, ff = gate_pre.shape
    tokens = n_dp * group
    chips = n_dp // 2
    nk = chips
    dk = d // nk
    cols = d // n_dp
    nf = 2
    vmem, hbm = pl.BlockSpec(memory_space=pltpu.VMEM), pl.BlockSpec(memory_space=pltpu.HBM)
    dma = pltpu.SemaphoreType.DMA
    pairs = [(nk, chips), (nk, 2, n_t), (nk, n_t), (2, n_dp), (2, 2, n_t), (2, nf, 7)]
    return pl.pallas_call(
        functools.partial(hidden_kernel, n_dp, n_t),
        out_shape=[jax.ShapeDtypeStruct((tokens, ff), BF16)] * 3
        + [jax.ShapeDtypeStruct((cols, tokens), BF16)] * 2,
        in_specs=[vmem, vmem, vmem, hbm, hbm, hbm],
        out_specs=[vmem] * 5,
        scratch_shapes=[
            pltpu.VMEM((nk, 2, n_t, chips, 2 * rows, dk // 2), BF16),
            pltpu.VMEM((n_dp, 2 * rows, cols // 2), BF16),
            pltpu.VMEM((n_t, n_dp, 2 * rows, cols // 2), BF16),
            pltpu.VMEM((n_t, n_dp, rows, 128), jnp.int32),
            pltpu.VMEM((2, nf, n_dp, group, ff // nf), BF16),
            pltpu.VMEM((d, ff), BF16),
            pltpu.VMEM((tokens, ff), F32),
            pltpu.VMEM((n_dp * n_t, rows, dk), F32),
            pltpu.VMEM((tokens, dk), BF16),
            pltpu.VMEM((tokens, cols), F32),
            pltpu.VMEM((n_dp * n_t, rows, 128), jnp.int32),
            pltpu.VMEM((n_dp, group, 128), F32),
        ]
        + [dma(shape) for shape in pairs for _ in range(2)]
        + [dma((nk,)), dma((2, nf))],
        compiler_params=pltpu.CompilerParams(
            collective_id=0, has_side_effects=True, vmem_limit_bytes=58 * 2**20
        ),
        cost_estimate=pl.CostEstimate(
            flops=2 * tokens * d * ff, bytes_accessed=2 * d * ff, transcendentals=tokens * ff
        ),
    )(acts, out_grad, segments, gate_pre, up_pre, down_weight)


def outer_kernel(acts_t, grads_t, gg, ug, wh, gate_out, up_out, down_out):
    gate_out[...] = jnp.dot(acts_t[...], gg[...], preferred_element_type=F32)
    up_out[...] = jnp.dot(acts_t[...], ug[...], preferred_element_type=F32)
    down_out[...] = jnp.dot(grads_t[...], wh[...], preferred_element_type=F32)


def outer_call(gg, ug, wh, acts_t, grads_t):
    cols, tokens = acts_t.shape
    ff = gg.shape[1]
    tf = tile_of(ff, 512)
    left = pl.BlockSpec((cols, tokens), lambda i: (0, 0))
    right = pl.BlockSpec((tokens, tf), lambda i: (0, i))
    return pl.pallas_call(
        outer_kernel,
        grid=(ff // tf,),
        out_shape=[jax.ShapeDtypeStruct((cols, ff), F32)] * 3,
        in_specs=[left, left, right, right, right],
        out_specs=[pl.BlockSpec((cols, tf), lambda i: (0, i))] * 3,
        compiler_params=pltpu.CompilerParams(vmem_limit_bytes=60 * 2**20),
        cost_estimate=pl.CostEstimate(
            flops=6 * tokens * cols * ff, bytes_accessed=12 * cols * ff, transcendentals=0
        ),
    )(acts_t, grads_t, gg, ug, wh)


def contract(left, right):
    return lax.dot_general(
        left, right, (((0,), (0,)), ((), ())), preferred_element_type=jnp.float32
    )


def token_weights(seg_groups):
    same = seg_groups[:, :, None] == seg_groups[:, None, :]
    return 1.0 / jnp.sum(same.astype(jnp.float32), axis=2).reshape(-1)


def body(acts, gate_pre, up_pre, out_grad, segments, down_weight):
    n_dp, n_t = lax.axis_size("dp"), lax.axis_size("tensor")
    rows, d = acts.shape
    if n_dp // 2 == 4:
        return tuple(
            outer_call(*hidden_call(n_dp, n_t, acts, gate_pre, up_pre, out_grad, segments, down_weight))
        )
    grad_all = lax.all_gather(out_grad, MESH, axis=0, tiled=True)
    gate_all = lax.all_gather(gate_pre, "dp", axis=0, tiled=True)
    up_all = lax.all_gather(up_pre, "dp", axis=0, tiled=True)
    seg_all = lax.all_gather(segments, MESH, axis=0, tiled=True)
    seg_all = seg_all.reshape(n_dp, n_t * rows)
    cols = d // n_dp
    mine = lax.all_to_all(acts, "dp", split_axis=1, concat_axis=0, tiled=True)
    mine = lax.all_gather(mine, "tensor", axis=0, tiled=False)
    mine = mine.reshape(n_t, n_dp, rows, cols).transpose(1, 0, 2, 3).reshape(-1, cols)
    me = lax.axis_index("dp")
    grad_mine = lax.dynamic_slice_in_dim(grad_all, me * cols, cols, axis=1)
    weights = token_weights(seg_all)[:, None]
    raw = jnp.dot(grad_all, down_weight, preferred_element_type=jnp.float32)
    gate = gate_all.astype(jnp.float32)
    up = up_all.astype(jnp.float32)
    sigma = jax.nn.sigmoid(gate)
    active = gate * sigma
    hidden_grad = weights * raw
    gate_grad = (hidden_grad * up * sigma * (1.0 + gate * (1.0 - sigma))).astype(jnp.bfloat16)
    up_grad = (hidden_grad * active).astype(jnp.bfloat16)
    weighted_hidden = (weights * active * up).astype(jnp.bfloat16)
    return contract(mine, gate_grad), contract(mine, up_grad), contract(grad_mine, weighted_hidden)


def solution(mesh):
    in_specs = (
        P(("dp", "tensor"), None),
        P("dp", "tensor"),
        P("dp", "tensor"),
        P(("dp", "tensor"), None),
        P("dp", "tensor"),
        P(None, "tensor"),
    )
    out_specs = (P("dp", "tensor"), P("dp", "tensor"), P("dp", "tensor"))
    return jax.shard_map(body, mesh=mesh, in_specs=in_specs, out_specs=out_specs, check_vma=False)
```

```python
import functools

import jax
import jax.numpy as jnp
from jax import lax
from jax.experimental import pallas as pl
from jax.experimental.pallas import tpu as pltpu
from jax.sharding import PartitionSpec as P

MESH = ("dp", "tensor")
F32, BF16 = jnp.float32, jnp.bfloat16
CORE, NEAR, FAR = 1, 2, 4


def tile_of(extent, most):
    return max(t for t in range(128, most + 1, 128) if extent % t == 0)


def hidden_kernel(
    n_dp, n_t,
    acts, grads, segs, gate_in, up_in, weight_in,
    gg_out, ug_out, wh_out, acts_t_out, grads_t_out,
    og, acts_cut, ac, sg, gu, wt, acc, lhs32, lhs16, own32, sg32, wgt,
    og_s, og_r, oz_s, oz_r, cut_s, cut_r, cl_s, cl_r, gu_s, gu_r, w_sem, own_sem,
):
    chips = n_dp // 2
    nk = chips
    rows, d = acts.shape
    dk = d // nk
    half = dk // 2
    group = n_t * rows
    ff = gate_in.shape[1]
    nf = gu.shape[1]
    fcut = ff // nf
    dp, z = lax.axis_index("dp"), lax.axis_index("tensor")
    core, chip = dp % 2, dp // 2

    def send(src, dst, s, r, to_dp, to_z):
        pltpu.make_async_remote_copy(
            src_ref=src, dst_ref=dst, send_sem=s, recv_sem=r,
            device_id=(to_dp, to_z), device_id_type=pl.DeviceIdType.MESH,
        ).start()

    def desc(ref, s, r):
        return pltpu.make_async_remote_copy(
            src_ref=ref, dst_ref=ref, send_sem=s, recv_sem=r,
            device_id=(dp ^ CORE, z), device_id_type=pl.DeviceIdType.MESH,
        )

    barrier = pltpu.get_barrier_semaphore()
    for rel in range(1, n_dp):
        pl.semaphore_signal(barrier, inc=1, device_id=(dp ^ rel, z), device_id_type=pl.DeviceIdType.MESH)

    for rel in range(1, n_t):
        pl.semaphore_signal(barrier, inc=1, device_id=(dp, (z + rel) % n_t), device_id_type=pl.DeviceIdType.MESH)

    w_copies = [
        pltpu.make_async_copy(weight_in.at[pl.ds(k * dk, dk)], wt.at[pl.ds(k * dk, dk)], w_sem.at[k])
        for k in range(nk)
    ]
    for c in w_copies:
        c.start()
    gu_in = (gate_in, up_in)
    own_copies = []
    for j in range(2):
        for f in range(nf):
            c = pltpu.make_async_copy(gu_in[j].at[:, pl.ds(f * fcut, fcut)], gu.at[j, f, dp], own_sem.at[j, f])
            c.start()
            own_copies.append(c)

    def stacked(x):
        w = x.shape[1] // 2
        return jnp.concatenate([x[:, :w], x[:, w:]], axis=0).astype(BF16)

    for k in range(nk):
        og[k, core, chip, z] = stacked(grads[:, k * dk:(k + 1) * dk].astype(F32))
    cols = d // n_dp
    for i in range(n_dp):
        acts_cut[i] = stacked(acts[:, i * cols:(i + 1) * cols].astype(F32))
    ac[z, dp] = acts_cut[dp]
    seg_row = jnp.broadcast_to(segs[...], (rows, rows))
    diag = lax.broadcasted_iota(jnp.int32, (rows, rows), 0) == lax.broadcasted_iota(jnp.int32, (rows, rows), 1)
    seg_col = jnp.sum(jnp.where(diag, seg_row, 0), axis=1, keepdims=True)
    sg[z, dp] = jnp.broadcast_to(seg_col, (rows, 128))

    pl.semaphore_wait(barrier, n_dp + n_t - 2)

    def start_lines():
        for k in range(nk):
            for rel in range(1, n_t):
                mine = og.at[k, core, chip, z]
                send(mine, mine, oz_s.at[k, rel], oz_r.at[k, rel], dp, (z + rel) % n_t)

    def start_cut():
        for rel in range(1, n_dp):
            send(sg.at[z, dp], sg.at[z, dp], cut_s.at[1, rel], cut_r.at[1, rel], dp ^ rel, z)
        for rel in range(1, n_dp):
            send(acts_cut.at[dp ^ rel], ac.at[z, dp], cut_s.at[0, rel], cut_r.at[0, rel], dp ^ rel, z)

    cut_parts = ((0, ac), (1, sg))

    def cut_lines():
        for i, ref in cut_parts:
            for rel in range(1, n_dp):
                desc(ref.at[z, dp ^ rel], cut_s.at[i, rel], cut_r.at[i, rel]).wait_recv()
            for rel in range(1, n_t):
                send(ref.at[z], ref.at[z], cl_s.at[i, rel], cl_r.at[i, rel], dp, (z + rel) % n_t)

    def cut_arrived():
        for i, ref in cut_parts:
            for rel in range(1, n_t):
                desc(ref.at[(z - rel + n_t) % n_t], cl_s.at[i, rel], cl_r.at[i, rel]).wait_recv()

    def gu_part(j, f):
        axes = (NEAR, FAR) if j == 0 else (FAR, NEAR)
        return (lambda x: gu.at[j, f, x]), gu_s.at[j, f], gu_r.at[j, f], axes

    def og_part(k):
        axes = (NEAR, FAR) if k % 2 == 0 else (FAR, NEAR)
        return (lambda x: og.at[k, x % 2, x // 2]), og_s.at[k], og_r.at[k], axes

    def start_plane(part):
        at, s, r, (a, b) = part
        for t, to in ((0, a), (1, b), (3, CORE)):
            send(at(dp), at(dp), s.at[t], r.at[t], dp ^ to, z)

    def hop(part, t):
        at, s, r, (a, b) = part
        slot = at(dp ^ (a, b, a ^ b)[t])
        desc(slot, s.at[t], r.at[t]).wait_recv()
        if t == 0:
            send(slot, slot, s.at[2], r.at[2], dp ^ b, z)
        send(slot, slot, s.at[4 + t], r.at[4 + t], dp ^ CORE, z)

    def from_sibling(part):
        at, s, r, (a, b) = part
        for t, slot in ((3, 0), (4, a), (5, b), (6, a ^ b)):
            desc(at(dp ^ CORE ^ slot), s.at[t], r.at[t]).wait_recv()

    def all_sent(part):
        at, s, r, axes = part
        for t in range(7):
            desc(at(dp), s.at[t], r.at[t]).wait_send()

    tf = tile_of(ff, 512)

    def matmul(k):
        from_sibling(og_part(k))

        def unpack(i, carry):
            c, q, s = i // (n_t * chips), (i // n_t) % chips, i % n_t
            x = og[k, c, q, s].astype(F32)
            to = (q * 2 + c) * n_t + s
            lhs32[to, :, 0:half] = x[:rows]
            lhs32[to, :, half:dk] = x[rows:]
            return carry

        lax.fori_loop(0, n_dp * n_t, unpack, 0)
        lhs16[...] = lhs32[...].reshape(n_dp * group, dk).astype(BF16)

        @pl.when(dp // 2 == k)
        def _():
            own32[...] = lhs32[:, :, pl.ds(pl.multiple_of((dp % 2) * half, half), half)].reshape(n_dp * group, half)

        w_copies[k].wait()

        def one(t, carry):
            at = pl.ds(pl.multiple_of(t * tf, tf), tf)
            part = jnp.dot(lhs16[...], wt[pl.ds(k * dk, dk), at], preferred_element_type=F32)
            if k == 0:
                acc[:, at] = part
            else:
                acc[:, at] += part
            return carry

        lax.fori_loop(0, ff // tf, one, 0)

    gus = [gu_part(j, f) for f in range(nf) for j in range(2)]
    ogs = [og_part(k) for k in range(nk)]
    start_lines()
    start_cut()
    for c in own_copies:
        c.wait()
    for part in gus:
        start_plane(part)
    for k in range(nk):
        for rel in range(1, n_t):
            desc(og.at[k, core, chip, (z - rel + n_t) % n_t], oz_s.at[k, rel], oz_r.at[k, rel]).wait_recv()
        start_plane(ogs[k])
    cut_lines()
    for t in range(2):
        for part in gus:
            hop(part, t)
        for part in ogs:
            hop(part, t)
    cut_arrived()

    def unpack_cut(i, carry):
        s, g = i // n_dp, i % n_dp
        x = ac[s, g].astype(F32)
        to = g * n_t + s
        lhs32[to, :, 0:cols // 2] = x[:rows]
        lhs32[to, :, cols // 2:cols] = x[rows:]
        sg32[to] = sg[s, g]
        return carry

    lax.fori_loop(0, n_dp * n_t, unpack_cut, 0)
    acts_t_out[...] = lhs32[:, :, 0:cols].reshape(n_dp * group, cols).T.astype(BF16)

    eye = lax.broadcasted_iota(jnp.int32, (group, group), 0) == lax.broadcasted_iota(jnp.int32, (group, group), 1)
    per = group // rows

    def weigh(g, carry):
        seg = sg32[pl.ds(g * per, per)].reshape(group, 128)[:, 0:1]
        wide = jnp.broadcast_to(seg, (group, group))
        row = jnp.sum(jnp.where(eye, wide, 0), axis=0, keepdims=True)
        count = jnp.sum((wide == row).astype(F32), axis=1, keepdims=True)
        wgt[g] = jnp.broadcast_to(1.0 / count, (group, 128))
        return carry

    lax.fori_loop(0, n_dp, weigh, 0)

    for part in gus:
        hop(part, 2)
    te = tile_of(fcut, 512)
    for f in range(nf):
        for j in range(2):
            from_sibling(gus[f * 2 + j])

        def element(i, carry, f=f):
            g, t = i // (fcut // te), i % (fcut // te)
            at = pl.ds(pl.multiple_of(t * te, te), te)
            here = pl.ds(pl.multiple_of(f * fcut + t * te, te), te)
            rows_at = pl.ds(pl.multiple_of(g * group, group), group)
            gate = gu[0, f, g, :, at].astype(F32)
            up = gu[1, f, g, :, at].astype(F32)
            w = wgt[g][:, 0:1]
            sigma = jax.nn.sigmoid(gate)
            active = gate * sigma
            gg_out[rows_at, here] = (w * up * (sigma + active * (1.0 - sigma))).astype(BF16)
            ug_out[rows_at, here] = (w * active).astype(BF16)
            wh_out[rows_at, here] = (w * active * up).astype(BF16)
            return carry

        lax.fori_loop(0, n_dp * (fcut // te), element, 0)
        if f == 0:
            for part in ogs:
                hop(part, 2)

    for k in range(nk):
        matmul(k)
    grads_t_out[...] = own32[...].T.astype(BF16)

    def scale(i, carry):
        at = pl.ds(pl.multiple_of(i * 128, 128), 128)
        raw = acc[:, at]
        gg_out[:, at] = (raw * gg_out[:, at].astype(F32)).astype(BF16)
        ug_out[:, at] = (raw * ug_out[:, at].astype(F32)).astype(BF16)
        return carry

    lax.fori_loop(0, ff // 128, scale, 0)

    for part in gus + ogs:
        all_sent(part)
    for k in range(nk):
        for rel in range(1, n_t):
            desc(og.at[k, core, chip, z], oz_s.at[k, rel], oz_r.at[k, rel]).wait_send()
    for rel in range(1, n_dp):
        desc(acts_cut.at[dp ^ rel], cut_s.at[0, rel], cut_r.at[0, rel]).wait_send()
        desc(sg.at[z, dp], cut_s.at[1, rel], cut_r.at[1, rel]).wait_send()
    for i, ref in cut_parts:
        for rel in range(1, n_t):
            desc(ref.at[z], cl_s.at[i, rel], cl_r.at[i, rel]).wait_send()


def hidden_call(n_dp, n_t, acts, gate_pre, up_pre, out_grad, segments, down_weight):
    rows, d = acts.shape
    group, ff = gate_pre.shape
    tokens = n_dp * group
    chips = n_dp // 2
    nk = chips
    dk = d // nk
    cols = d // n_dp
    nf = 2
    vmem, hbm = pl.BlockSpec(memory_space=pltpu.VMEM), pl.BlockSpec(memory_space=pltpu.HBM)
    dma = pltpu.SemaphoreType.DMA
    pairs = [(nk, 7), (nk, n_t), (2, n_dp), (2, n_t), (2, nf, 7)]
    return pl.pallas_call(
        functools.partial(hidden_kernel, n_dp, n_t),
        out_shape=[jax.ShapeDtypeStruct((tokens, ff), BF16)] * 3
        + [jax.ShapeDtypeStruct((cols, tokens), BF16)] * 2,
        in_specs=[vmem, vmem, vmem, hbm, hbm, hbm],
        out_specs=[vmem] * 5,
        scratch_shapes=[
            pltpu.VMEM((nk, 2, chips, n_t, 2 * rows, dk // 2), BF16),
            pltpu.VMEM((n_dp, 2 * rows, cols // 2), BF16),
            pltpu.VMEM((n_t, n_dp, 2 * rows, cols // 2), BF16),
            pltpu.VMEM((n_t, n_dp, rows, 128), jnp.int32),
            pltpu.VMEM((2, nf, n_dp, group, ff // nf), BF16),
            pltpu.VMEM((d, ff), BF16),
            pltpu.VMEM((tokens, ff), F32),
            pltpu.VMEM((n_dp * n_t, rows, dk), F32),
            pltpu.VMEM((tokens, dk), BF16),
            pltpu.VMEM((tokens, cols), F32),
            pltpu.VMEM((n_dp * n_t, rows, 128), jnp.int32),
            pltpu.VMEM((n_dp, group, 128), F32),
        ]
        + [dma(shape) for shape in pairs for _ in range(2)]
        + [dma((nk,)), dma((2, nf))],
        compiler_params=pltpu.CompilerParams(
            collective_id=0, has_side_effects=True, vmem_limit_bytes=58 * 2**20
        ),
        cost_estimate=pl.CostEstimate(
            flops=2 * tokens * d * ff, bytes_accessed=2 * d * ff, transcendentals=tokens * ff
        ),
    )(acts, out_grad, segments, gate_pre, up_pre, down_weight)


def outer_kernel(acts_t, grads_t, gg, ug, wh, gate_out, up_out, down_out):
    gate_out[...] = jnp.dot(acts_t[...], gg[...], preferred_element_type=F32)
    up_out[...] = jnp.dot(acts_t[...], ug[...], preferred_element_type=F32)
    down_out[...] = jnp.dot(grads_t[...], wh[...], preferred_element_type=F32)


def outer_call(gg, ug, wh, acts_t, grads_t):
    cols, tokens = acts_t.shape
    ff = gg.shape[1]
    tf = tile_of(ff, 512)
    left = pl.BlockSpec((cols, tokens), lambda i: (0, 0))
    right = pl.BlockSpec((tokens, tf), lambda i: (0, i))
    return pl.pallas_call(
        outer_kernel,
        grid=(ff // tf,),
        out_shape=[jax.ShapeDtypeStruct((cols, ff), F32)] * 3,
        in_specs=[left, left, right, right, right],
        out_specs=[pl.BlockSpec((cols, tf), lambda i: (0, i))] * 3,
        compiler_params=pltpu.CompilerParams(vmem_limit_bytes=60 * 2**20),
        cost_estimate=pl.CostEstimate(
            flops=6 * tokens * cols * ff, bytes_accessed=12 * cols * ff, transcendentals=0
        ),
    )(acts_t, grads_t, gg, ug, wh)


def contract(left, right):
    return lax.dot_general(
        left, right, (((0,), (0,)), ((), ())), preferred_element_type=jnp.float32
    )


def token_weights(seg_groups):
    same = seg_groups[:, :, None] == seg_groups[:, None, :]
    return 1.0 / jnp.sum(same.astype(jnp.float32), axis=2).reshape(-1)


def body(acts, gate_pre, up_pre, out_grad, segments, down_weight):
    n_dp, n_t = lax.axis_size("dp"), lax.axis_size("tensor")
    rows, d = acts.shape
    if n_dp // 2 == 4:
        return tuple(
            outer_call(*hidden_call(n_dp, n_t, acts, gate_pre, up_pre, out_grad, segments, down_weight))
        )
    grad_all = lax.all_gather(out_grad, MESH, axis=0, tiled=True)
    gate_all = lax.all_gather(gate_pre, "dp", axis=0, tiled=True)
    up_all = lax.all_gather(up_pre, "dp", axis=0, tiled=True)
    seg_all = lax.all_gather(segments, MESH, axis=0, tiled=True)
    seg_all = seg_all.reshape(n_dp, n_t * rows)
    cols = d // n_dp
    mine = lax.all_to_all(acts, "dp", split_axis=1, concat_axis=0, tiled=True)
    mine = lax.all_gather(mine, "tensor", axis=0, tiled=False)
    mine = mine.reshape(n_t, n_dp, rows, cols).transpose(1, 0, 2, 3).reshape(-1, cols)
    me = lax.axis_index("dp")
    grad_mine = lax.dynamic_slice_in_dim(grad_all, me * cols, cols, axis=1)
    weights = token_weights(seg_all)[:, None]
    raw = jnp.dot(grad_all, down_weight, preferred_element_type=jnp.float32)
    gate = gate_all.astype(jnp.float32)
    up = up_all.astype(jnp.float32)
    sigma = jax.nn.sigmoid(gate)
    active = gate * sigma
    hidden_grad = weights * raw
    gate_grad = (hidden_grad * up * sigma * (1.0 + gate * (1.0 - sigma))).astype(jnp.bfloat16)
    up_grad = (hidden_grad * active).astype(jnp.bfloat16)
    weighted_hidden = (weights * active * up).astype(jnp.bfloat16)
    return contract(mine, gate_grad), contract(mine, up_grad), contract(grad_mine, weighted_hidden)


def solution(mesh):
    in_specs = (
        P(("dp", "tensor"), None),
        P("dp", "tensor"),
        P("dp", "tensor"),
        P(("dp", "tensor"), None),
        P("dp", "tensor"),
        P(None, "tensor"),
    )
    out_specs = (P("dp", "tensor"), P("dp", "tensor"), P("dp", "tensor"))
    return jax.shard_map(body, mesh=mesh, in_specs=in_specs, out_specs=out_specs, check_vma=False)
```

```python
import functools

import jax
import jax.numpy as jnp
from jax import lax
from jax.experimental import pallas as pl
from jax.experimental.pallas import tpu as pltpu
from jax.sharding import PartitionSpec as P

MESH = ("dp", "tensor")
F32, BF16 = jnp.float32, jnp.bfloat16
CORE, NEAR, FAR = 1, 2, 4


def tile_of(extent, most):
    return max(t for t in range(128, most + 1, 128) if extent % t == 0)


def hidden_kernel(
    n_dp, n_t,
    acts, grads, segs, gate_in, up_in, weight_in,
    gg_out, ug_out, wh_out, acts_t_out, grads_t_out,
    og, acts_cut, ac, sg, gu, wt, acc, lhs32, lhs16, own32, sg32, wgt,
    og_s, og_r, line_s, line_r, sib_s, sib_r, cut_s, cut_r, cl_s, cl_r, gu_s, gu_r, w_sem, own_sem,
):
    chips = n_dp // 2
    nk = chips
    rows, d = acts.shape
    dk = d // nk
    half = dk // 2
    group = n_t * rows
    ff = gate_in.shape[1]
    nf = gu.shape[1]
    fcut = ff // nf
    dp, z = lax.axis_index("dp"), lax.axis_index("tensor")
    core, chip = dp % 2, dp // 2

    def send(src, dst, s, r, to_dp, to_z):
        pltpu.make_async_remote_copy(
            src_ref=src, dst_ref=dst, send_sem=s, recv_sem=r,
            device_id=(to_dp, to_z), device_id_type=pl.DeviceIdType.MESH,
        ).start()

    def desc(ref, s, r):
        return pltpu.make_async_remote_copy(
            src_ref=ref, dst_ref=ref, send_sem=s, recv_sem=r,
            device_id=(dp ^ CORE, z), device_id_type=pl.DeviceIdType.MESH,
        )

    barrier = pltpu.get_barrier_semaphore()
    for rel in range(1, n_dp):
        pl.semaphore_signal(barrier, inc=1, device_id=(dp ^ rel, z), device_id_type=pl.DeviceIdType.MESH)

    @pl.when(z > 0)
    def _():
        pl.semaphore_signal(barrier, inc=1, device_id=(dp, z - 1), device_id_type=pl.DeviceIdType.MESH)

    @pl.when(z < n_t - 1)
    def _():
        pl.semaphore_signal(barrier, inc=1, device_id=(dp, z + 1), device_id_type=pl.DeviceIdType.MESH)

    w_copies = [
        pltpu.make_async_copy(weight_in.at[pl.ds(k * dk, dk)], wt.at[pl.ds(k * dk, dk)], w_sem.at[k])
        for k in range(nk)
    ]
    gu_in = (gate_in, up_in)
    own_copies = []
    for j in range(2):
        for f in range(nf):
            c = pltpu.make_async_copy(gu_in[j].at[:, pl.ds(f * fcut, fcut)], gu.at[j, f, dp], own_sem.at[j, f])
            c.start()
            own_copies.append(c)

    def stacked(x):
        w = x.shape[1] // 2
        return jnp.concatenate([x[:, :w], x[:, w:]], axis=0).astype(BF16)

    for k in range(nk):
        og[k, core, z, chip] = stacked(grads[:, k * dk:(k + 1) * dk].astype(F32))
    cols = d // n_dp
    for i in range(n_dp):
        acts_cut[i] = stacked(acts[:, i * cols:(i + 1) * cols].astype(F32))
    ac[z, dp] = acts_cut[dp]
    seg_row = jnp.broadcast_to(segs[...], (rows, rows))
    diag = lax.broadcasted_iota(jnp.int32, (rows, rows), 0) == lax.broadcasted_iota(jnp.int32, (rows, rows), 1)
    seg_col = jnp.sum(jnp.where(diag, seg_row, 0), axis=1, keepdims=True)
    sg[z, dp] = jnp.broadcast_to(seg_col, (rows, 128))

    pl.semaphore_wait(barrier, n_dp - 1 + (z > 0).astype(jnp.int32) + (z < n_t - 1).astype(jnp.int32))

    for k in range(nk):
        for rel in range(1, chips):
            mine = og.at[k, core, z, chip]
            send(mine, mine, og_s.at[k, rel], og_r.at[k, rel], dp ^ (2 * rel), z)

    def gu_axes(j):
        return (NEAR, FAR) if j == 0 else (FAR, NEAR)

    def start_gu():
        for f in range(nf):
            for j in range(2):
                own_copies[j * nf + f].wait()
            for t in range(2):
                for j in range(2):
                    mine = gu.at[j, f, dp]
                    send(mine, mine, gu_s.at[j, f, t], gu_r.at[j, f, t], dp ^ gu_axes(j)[t], z)
            for j in range(2):
                mine = gu.at[j, f, dp]
                send(mine, mine, gu_s.at[j, f, 3], gu_r.at[j, f, 3], dp ^ CORE, z)

    def gu_hop(j, f, t):
        a, b = gu_axes(j)
        slot = gu.at[j, f, dp ^ (a, b, a ^ b)[t]]
        desc(slot, gu_s.at[j, f, t], gu_r.at[j, f, t]).wait_recv()
        if t == 0:
            send(slot, slot, gu_s.at[j, f, 2], gu_r.at[j, f, 2], dp ^ b, z)
        send(slot, slot, gu_s.at[j, f, 4 + t], gu_r.at[j, f, 4 + t], dp ^ CORE, z)

    def start_cut():
        for rel in range(1, n_dp):
            send(acts_cut.at[dp ^ rel], ac.at[z, dp], cut_s.at[0, rel], cut_r.at[0, rel], dp ^ rel, z)
            send(sg.at[z, dp], sg.at[z, dp], cut_s.at[1, rel], cut_r.at[1, rel], dp ^ rel, z)

    def line_parts(k):
        if k < nk:
            return [(lambda s: og.at[k, core, s], line_s.at[k], line_r.at[k])]
        return [(lambda s: ac.at[s], cl_s.at[0], cl_r.at[0]), (lambda s: sg.at[s], cl_s.at[1], cl_r.at[1])]

    def pass_on(k, s):
        if k < nk:
            plane = og.at[k, core, s]
            send(plane, plane, sib_s.at[k, s], sib_r.at[k, s], dp ^ CORE, z)

    def step(k, h):
        if h == 0:
            if k < nk:
                for rel in range(1, chips):
                    desc(og.at[k, core, z, chip ^ rel], og_s.at[k, rel], og_r.at[k, rel]).wait_recv()
            else:
                for rel in range(1, n_dp):
                    desc(ac.at[z, dp ^ rel], cut_s.at[0, rel], cut_r.at[0, rel]).wait_recv()
                    desc(sg.at[z, dp ^ rel], cut_s.at[1, rel], cut_r.at[1, rel]).wait_recv()
        for way in range(2):
            sign = 1 - 2 * way
            src = z - sign * h
            nxt = z + sign
            valid = (src >= 0) & (src < n_t)

            def arrive(way=way, src=src, nxt=nxt):
                if h:
                    for at, s, r in line_parts(k):
                        desc(at(src), s.at[way, h], r.at[way, h]).wait_recv()

                if h + 1 < n_t:
                    @pl.when((nxt >= 0) & (nxt < n_t))
                    def _():
                        for at, s, r in line_parts(k):
                            send(at(src), at(src), s.at[way, h + 1], r.at[way, h + 1], dp, nxt)

                if h or way == 0:
                    pass_on(k, src)

            if h:
                pl.when(valid)(arrive)
            else:
                arrive()

    tf = tile_of(ff, 512)

    def matmul(k):
        for s in range(n_t):
            desc(og.at[k, 1 - core, s], sib_s.at[k, s], sib_r.at[k, s]).wait_recv()

        def unpack(i, carry):
            c, s, q = i // (n_t * chips), (i // chips) % n_t, i % chips
            x = og[k, c, s, q].astype(F32)
            to = (q * 2 + c) * n_t + s
            lhs32[to, :, 0:half] = x[:rows]
            lhs32[to, :, half:dk] = x[rows:]
            return carry

        lax.fori_loop(0, n_dp * n_t, unpack, 0)
        lhs16[...] = lhs32[...].reshape(n_dp * group, dk).astype(BF16)

        @pl.when(dp // 2 == k)
        def _():
            own32[...] = lhs32[:, :, pl.ds(pl.multiple_of((dp % 2) * half, half), half)].reshape(n_dp * group, half)

        w_copies[k].wait()

        def one(t, carry):
            at = pl.ds(pl.multiple_of(t * tf, tf), tf)
            part = jnp.dot(lhs16[...], wt[pl.ds(k * dk, dk), at], preferred_element_type=F32)
            if k == 0:
                acc[:, at] = part
            else:
                acc[:, at] += part
            return carry

        lax.fori_loop(0, ff // tf, one, 0)

    start_cut()
    start_gu()
    for c in w_copies:
        c.start()
    for s in range(nk + n_t):
        for h in range(n_t):
            if 0 <= s - h <= nk:
                step(s - h, h)
        if s == n_t - 1:
            for f in range(nf):
                for j in range(2):
                    gu_hop(j, f, 0)
        if s == n_t:
            for f in range(nf):
                for j in range(2):
                    gu_hop(j, f, 1)
        if 0 <= s - (n_t - 1) < nk:
            matmul(s - (n_t - 1))
    grads_t_out[...] = own32[...].T.astype(BF16)

    def unpack_cut(i, carry):
        s, g = i // n_dp, i % n_dp
        x = ac[s, g].astype(F32)
        to = g * n_t + s
        lhs32[to, :, 0:cols // 2] = x[:rows]
        lhs32[to, :, cols // 2:cols] = x[rows:]
        sg32[to] = sg[s, g]
        return carry

    lax.fori_loop(0, n_dp * n_t, unpack_cut, 0)
    acts_t_out[...] = lhs32[:, :, 0:cols].reshape(n_dp * group, cols).T.astype(BF16)

    eye = lax.broadcasted_iota(jnp.int32, (group, group), 0) == lax.broadcasted_iota(jnp.int32, (group, group), 1)
    per = group // rows

    def weigh(g, carry):
        seg = sg32[pl.ds(g * per, per)].reshape(group, 128)[:, 0:1]
        wide = jnp.broadcast_to(seg, (group, group))
        row = jnp.sum(jnp.where(eye, wide, 0), axis=0, keepdims=True)
        count = jnp.sum((wide == row).astype(F32), axis=1, keepdims=True)
        wgt[g] = jnp.broadcast_to(1.0 / count, (group, 128))
        return carry

    lax.fori_loop(0, n_dp, weigh, 0)

    for f in range(nf):
        for j in range(2):
            gu_hop(j, f, 2)
    for f in range(nf):
        for j in range(2):
            a, b = gu_axes(j)
            for t, slot in ((3, 0), (4, a), (5, b), (6, a ^ b)):
                desc(gu.at[j, f, dp ^ CORE ^ slot], gu_s.at[j, f, t], gu_r.at[j, f, t]).wait_recv()
    te = tile_of(fcut, 512)
    for f in range(nf):
        def element(i, carry, f=f):
            g, t = i // (fcut // te), i % (fcut // te)
            at = pl.ds(pl.multiple_of(t * te, te), te)
            here = pl.ds(pl.multiple_of(f * fcut + t * te, te), te)
            rows_at = pl.ds(pl.multiple_of(g * group, group), group)
            gate = gu[0, f, g, :, at].astype(F32)
            up = gu[1, f, g, :, at].astype(F32)
            w = wgt[g][:, 0:1]
            raw = acc[rows_at, here]
            sigma = jax.nn.sigmoid(gate)
            active = gate * sigma
            hid = w * raw
            gg_out[rows_at, here] = (hid * up * (sigma + active * (1.0 - sigma))).astype(BF16)
            ug_out[rows_at, here] = (hid * active).astype(BF16)
            wh_out[rows_at, here] = (w * active * up).astype(BF16)
            return carry

        lax.fori_loop(0, n_dp * (fcut // te), element, 0)

    for k in range(nk):
        for rel in range(1, chips):
            desc(og.at[k, core, z, chip], og_s.at[k, rel], og_r.at[k, rel]).wait_send()
        for s in range(n_t):
            desc(og.at[k, core, s], sib_s.at[k, s], sib_r.at[k, s]).wait_send()
    for rel in range(1, n_dp):
        desc(acts_cut.at[dp ^ rel], cut_s.at[0, rel], cut_r.at[0, rel]).wait_send()
        desc(sg.at[z, dp], cut_s.at[1, rel], cut_r.at[1, rel]).wait_send()
    for k in range(nk + 1):
        for h in range(1, n_t):
            for way in range(2):
                sign = 1 - 2 * way
                src, nxt = z - sign * (h - 1), z + sign

                @pl.when((src >= 0) & (src < n_t) & (nxt >= 0) & (nxt < n_t))
                def _():
                    for at, s, r in line_parts(k):
                        desc(at(src), s.at[way, h], r.at[way, h]).wait_send()
    for f in range(nf):
        for j in range(2):
            for t in range(7):
                desc(gu.at[j, f, dp], gu_s.at[j, f, t], gu_r.at[j, f, t]).wait_send()


def hidden_call(n_dp, n_t, acts, gate_pre, up_pre, out_grad, segments, down_weight):
    rows, d = acts.shape
    group, ff = gate_pre.shape
    tokens = n_dp * group
    chips = n_dp // 2
    nk = chips
    dk = d // nk
    cols = d // n_dp
    nf = 2
    vmem, hbm = pl.BlockSpec(memory_space=pltpu.VMEM), pl.BlockSpec(memory_space=pltpu.HBM)
    dma = pltpu.SemaphoreType.DMA
    pairs = [(nk, chips), (nk, 2, n_t), (nk, n_t), (2, n_dp), (2, 2, n_t), (2, nf, 7)]
    return pl.pallas_call(
        functools.partial(hidden_kernel, n_dp, n_t),
        out_shape=[jax.ShapeDtypeStruct((tokens, ff), BF16)] * 3
        + [jax.ShapeDtypeStruct((cols, tokens), BF16)] * 2,
        in_specs=[vmem, vmem, vmem, hbm, hbm, hbm],
        out_specs=[vmem] * 5,
        scratch_shapes=[
            pltpu.VMEM((nk, 2, n_t, chips, 2 * rows, dk // 2), BF16),
            pltpu.VMEM((n_dp, 2 * rows, cols // 2), BF16),
            pltpu.VMEM((n_t, n_dp, 2 * rows, cols // 2), BF16),
            pltpu.VMEM((n_t, n_dp, rows, 128), jnp.int32),
            pltpu.VMEM((2, nf, n_dp, group, ff // nf), BF16),
            pltpu.VMEM((d, ff), BF16),
            pltpu.VMEM((tokens, ff), F32),
            pltpu.VMEM((n_dp * n_t, rows, dk), F32),
            pltpu.VMEM((tokens, dk), BF16),
            pltpu.VMEM((tokens, cols), F32),
            pltpu.VMEM((n_dp * n_t, rows, 128), jnp.int32),
            pltpu.VMEM((n_dp, group, 128), F32),
        ]
        + [dma(shape) for shape in pairs for _ in range(2)]
        + [dma((nk,)), dma((2, nf))],
        compiler_params=pltpu.CompilerParams(
            collective_id=0, has_side_effects=True, vmem_limit_bytes=58 * 2**20
        ),
        cost_estimate=pl.CostEstimate(
            flops=2 * tokens * d * ff, bytes_accessed=2 * d * ff, transcendentals=tokens * ff
        ),
    )(acts, out_grad, segments, gate_pre, up_pre, down_weight)


def outer_kernel(acts_t, grads_t, gg, ug, wh, gate_out, up_out, down_out):
    gate_out[...] = jnp.dot(acts_t[...], gg[...], preferred_element_type=F32)
    up_out[...] = jnp.dot(acts_t[...], ug[...], preferred_element_type=F32)
    down_out[...] = jnp.dot(grads_t[...], wh[...], preferred_element_type=F32)


def outer_call(gg, ug, wh, acts_t, grads_t):
    cols, tokens = acts_t.shape
    ff = gg.shape[1]
    tf = tile_of(ff, 512)
    left = pl.BlockSpec((cols, tokens), lambda i: (0, 0))
    right = pl.BlockSpec((tokens, tf), lambda i: (0, i))
    return pl.pallas_call(
        outer_kernel,
        grid=(ff // tf,),
        out_shape=[jax.ShapeDtypeStruct((cols, ff), F32)] * 3,
        in_specs=[left, left, right, right, right],
        out_specs=[pl.BlockSpec((cols, tf), lambda i: (0, i))] * 3,
        compiler_params=pltpu.CompilerParams(vmem_limit_bytes=60 * 2**20),
        cost_estimate=pl.CostEstimate(
            flops=6 * tokens * cols * ff, bytes_accessed=12 * cols * ff, transcendentals=0
        ),
    )(acts_t, grads_t, gg, ug, wh)


def contract(left, right):
    return lax.dot_general(
        left, right, (((0,), (0,)), ((), ())), preferred_element_type=jnp.float32
    )


def token_weights(seg_groups):
    same = seg_groups[:, :, None] == seg_groups[:, None, :]
    return 1.0 / jnp.sum(same.astype(jnp.float32), axis=2).reshape(-1)


def body(acts, gate_pre, up_pre, out_grad, segments, down_weight):
    n_dp, n_t = lax.axis_size("dp"), lax.axis_size("tensor")
    rows, d = acts.shape
    if n_dp // 2 == 4:
        return tuple(
            outer_call(*hidden_call(n_dp, n_t, acts, gate_pre, up_pre, out_grad, segments, down_weight))
        )
    grad_all = lax.all_gather(out_grad, MESH, axis=0, tiled=True)
    gate_all = lax.all_gather(gate_pre, "dp", axis=0, tiled=True)
    up_all = lax.all_gather(up_pre, "dp", axis=0, tiled=True)
    seg_all = lax.all_gather(segments, MESH, axis=0, tiled=True)
    seg_all = seg_all.reshape(n_dp, n_t * rows)
    cols = d // n_dp
    mine = lax.all_to_all(acts, "dp", split_axis=1, concat_axis=0, tiled=True)
    mine = lax.all_gather(mine, "tensor", axis=0, tiled=False)
    mine = mine.reshape(n_t, n_dp, rows, cols).transpose(1, 0, 2, 3).reshape(-1, cols)
    me = lax.axis_index("dp")
    grad_mine = lax.dynamic_slice_in_dim(grad_all, me * cols, cols, axis=1)
    weights = token_weights(seg_all)[:, None]
    raw = jnp.dot(grad_all, down_weight, preferred_element_type=jnp.float32)
    gate = gate_all.astype(jnp.float32)
    up = up_all.astype(jnp.float32)
    sigma = jax.nn.sigmoid(gate)
    active = gate * sigma
    hidden_grad = weights * raw
    gate_grad = (hidden_grad * up * sigma * (1.0 + gate * (1.0 - sigma))).astype(jnp.bfloat16)
    up_grad = (hidden_grad * active).astype(jnp.bfloat16)
    weighted_hidden = (weights * active * up).astype(jnp.bfloat16)
    return contract(mine, gate_grad), contract(mine, up_grad), contract(grad_mine, weighted_hidden)


def solution(mesh):
    in_specs = (
        P(("dp", "tensor"), None),
        P("dp", "tensor"),
        P("dp", "tensor"),
        P(("dp", "tensor"), None),
        P("dp", "tensor"),
        P(None, "tensor"),
    )
    out_specs = (P("dp", "tensor"), P("dp", "tensor"), P("dp", "tensor"))
    return jax.shard_map(body, mesh=mesh, in_specs=in_specs, out_specs=out_specs, check_vma=False)
```
